32 devices in a mesh: dp: 8 (over y, x, core), expert: 4 (over z).
Axes of the slice: x: 2, y: 2, z: 4, core: 2. Of those that a mesh axis runs over, the one named last changes fastest.
Arguments:
- grad_rows: bfloat16 [4096, 3584], P(('dp', 'expert')), may hold values from -6 to 6
- grad_exponent: int32 [4096, 28], P(('dp', 'expert')), may hold values from 0 to 3
- gate: bfloat16 [4096], P(('dp', 'expert')), may hold values from 0.049804688 to 1
- routing: int32 [4096, 1], P(('dp', 'expert')), may hold values from 0 to 3; in each aligned block of 128 rows (0 to 127, 128 to 255, ...) at most 34 rows name the same one
- saved_hidden: bfloat16 [8, 4, 136, 1024], P('dp', 'expert'), may hold values from -6 to 6
- down_weight: bfloat16 [4, 1024, 3584], P('expert'), may hold values from -0.1875 to 0.1875
Outputs:
- hidden_grad: bfloat16 [8, 4, 136, 1024], P('dp', 'expert')
- weight_grad: float32 [4, 1024, 3584], P('expert', 'dp')
- gate_grad: float32 [4096], P(('dp', 'expert'))
The draws below stay inside these ranges and needn't reach their ends.
Inputs may be any that keep to these rules, and one draw needn't show every extreme that they name: `routing`: within one device's 128 rows no expert is named more than 34 times; in some device's rows one expert is named exactly 34 times.
All inputs are finite; a program needn't handle non-finite values.
Results may differ from the reference program's by a relative error of at most 0.0095.
Values may be sent and summed in bfloat16 or wider, within the bound.
A program may use at most 64 MiB of HBM per device.

```python
import math
import jax
import jax.numpy as jnp
import numpy as np
from jax import lax

D = 3584
H = 1024
BLK = 128
TOK_DEV = 128
EXPERTS = 4
CAP = 34
SLOTS = 136
TOKENS = 4096
N_DP = 8
N_EXPERT = 4


def with_ends(values, key, least, largest):
    extent = values.shape
    index_at = [jax.random.randint(jax.random.fold_in(key, axis), (), 0, extent[axis]) for axis in range(len(extent))]
    values = values.at[tuple(index_at)].set(least)
    longest = extent.index(max(extent))
    index_at[longest] = (index_at[longest] + 1) % extent[longest]
    return values.at[tuple(index_at)].set(largest)


def steps_of(key, dims, split, low, top_value):
    gain = 1.0
    for dim, parts in split:
        heights = jax.random.uniform(jax.random.fold_in(jax.random.fold_in(key, 6), dim), (parts,), jnp.float32, low / len(split), top_value / len(split))
        gain = gain * jnp.repeat(jnp.exp(heights), dims[dim] // parts).reshape((-1,) + (1,) * (len(dims) - 1 - dim))
    return gain


def routed_block(own_key, own, number, rows, amount, top, most, skew):
    order = jax.random.permutation(own_key, amount)
    heavy_load, ordinary = portions_of(amount, rows * top, most, skew, True), portions_of(amount, rows * top, most, skew, False)
    places = jnp.arange(amount)

    def named(sizes, turn):
        used = int((sizes > 0).sum())
        fixed = max(1, used // 4)
        passed = fixed + (places - fixed + turn * (used - fixed)) % max(1, amount - fixed)
        return jnp.zeros((amount,), jnp.int32).at[order[jnp.where(places < fixed, places, passed)]].set(jnp.asarray(sizes, jnp.int32))

    sizes = jnp.where(number % 4 == 0, named(heavy_load, number // 4), named(ordinary, number - number // 4 - 1))
    mixed = jax.random.permutation(jax.random.fold_in(own, 3), amount)
    source_of, taker = mixed[0:amount // 2 * 2:2], mixed[1:amount // 2 * 2:2]
    margin = jnp.minimum(sizes[source_of] - 1, most - sizes[taker]) // 2
    margin = jnp.where((source_of == order[0]) | (taker == order[0]) | (sizes[taker] == 0), 0, jnp.maximum(margin, 0))
    passed = jax.random.randint(jax.random.fold_in(own, 4), (amount // 2,), 0, 1 << 20) % (margin + 1)
    sizes = sizes.at[source_of].add(-passed).at[taker].add(passed)
    labels = jnp.searchsorted(jnp.cumsum(sizes), jnp.arange(rows * top), side="right").astype(jnp.int32)
    listing = labels.reshape(top, rows).T
    listing = listing[jax.random.permutation(jax.random.fold_in(own, 1), rows)]
    turn = jax.random.randint(jax.random.fold_in(own, 2), (rows, 1), 0, top)
    return jnp.take_along_axis(listing, (jnp.arange(top)[None, :] + turn) % top, axis=1)


def portions_of(amount, total, bound, skew, full):
    loads = [(1 << 20) // math.isqrt(rank ** skew) + 1 for rank in range(1, amount + 1)]
    largest = bound if full else min(bound, max(-(-total // amount), total * loads[0] // sum(loads)))
    least = 1 if total - largest >= amount - 1 else 0
    given, rest = [largest] + [least] * (amount - 1), total - largest - least * (amount - 1)
    while rest > 0:
        free = [i for i in range(1, amount) if given[i] < largest] or [i for i in range(1, amount) if given[i] < bound]
        pool, left = sum([loads[i] for i in free]), rest
        for i in free:
            more = min(bound - given[i], max(1, left * loads[i] // pool), rest)
            given[i] = given[i] + more
            rest = rest - more
    return np.array(given)


def noise(own_key, dims, scale, reach, cuts=(), held_as=jnp.bfloat16):
    entries = scale * jax.random.normal(own_key, dims, jnp.float32)
    if cuts:
        entries = entries * steps_of(own_key, dims, cuts, -0.22, 0.18)
    return jnp.clip(entries, -reach, reach).astype(held_as)


def setup_inputs(seed: int = 0) -> dict:
    keys = jax.random.split(jax.random.key(seed), 7)
    grad_rows = noise(keys[0], (TOKENS, D), 1.0, 6.0, ((0, 32),))
    grad_exponent = with_ends(jax.random.randint(keys[1], (TOKENS, D // BLK), 0, 4), jax.random.fold_in(keys[1], 1), 0, 3).astype(jnp.int32)
    gate = jnp.clip(jnp.exp(math.log(1.0) - 2.9996462 * jax.random.uniform(keys[2], (TOKENS,), jnp.float32) ** steps_of(keys[2], (TOKENS,), ((0, 32),), -0.2, 0.2)), 0.049804688, 1.0).astype(jnp.bfloat16)
    routing_keys = jax.random.split(jax.random.fold_in(keys[3], 1), TOKENS // TOK_DEV)
    routing_turns = jax.random.permutation(jax.random.fold_in(keys[3], 3), TOKENS // TOK_DEV)
    routing = jax.vmap(lambda own, number: routed_block(jax.random.fold_in(keys[3], 2), own, number, TOK_DEV, EXPERTS, 1, CAP, 2))(routing_keys, routing_turns).reshape((TOKENS, 1))
    saved_hidden = noise(keys[4], (N_DP, EXPERTS, SLOTS, H), 1.0, 6.0, ((0, 8), (1, 4)))
    down_weight = noise(keys[5], (EXPERTS, H, D), H ** -0.5, 0.1875, ((0, 4),))
    return {"grad_rows": grad_rows, "grad_exponent": grad_exponent, "gate": gate, "routing": routing, "saved_hidden": saved_hidden, "down_weight": down_weight}


def slot_table(route, experts, cap):
    onehot = (route[:, None] == jnp.arange(experts, dtype=jnp.int32)[None, :]).astype(jnp.int32)
    before = jnp.cumsum(onehot, axis=0) - onehot
    rank = jnp.sum(before * onehot, axis=1).astype(jnp.int32)
    slot = route * cap + rank
    return slot[:, None] == jnp.arange(experts * cap, dtype=jnp.int32)[None, :]


def scaled_rows(rows, exponent):
    count, width = rows.shape
    blocks = exponent.shape[1]
    factor = 1.0 / jnp.left_shift(jnp.ones_like(exponent), exponent).astype(jnp.float32)
    scaled = rows.astype(jnp.float32).reshape(count, blocks, width // blocks) * factor[:, :, None]
    return scaled.reshape(count, width).astype(jnp.bfloat16)


def reference(grad_rows, grad_exponent, gate, routing, saved_hidden, down_weight):
    dy_all = scaled_rows(grad_rows, grad_exponent).reshape(N_DP, N_EXPERT, TOK_DEV, D)
    gate_all = gate.reshape(N_DP, N_EXPERT, TOK_DEV)
    route_all = routing[:, 0].reshape(N_DP, N_EXPERT, TOK_DEV)

    def per_expert(inputs):
        rows, gates, hidden, weight = inputs
        raw = jnp.dot(rows, weight.T, preferred_element_type=jnp.float32)
        hidden_grad = (gates.astype(jnp.float32)[:, None] * raw).astype(jnp.bfloat16)
        output = jnp.dot(hidden, weight, preferred_element_type=jnp.float32)
        slot_grad = jnp.sum(rows.astype(jnp.float32) * output, axis=1)
        weighted = (gates.astype(jnp.float32)[:, None] * rows.astype(jnp.float32)).astype(jnp.bfloat16)
        partial_grad = jnp.dot(hidden.T, weighted, preferred_element_type=jnp.float32).astype(jnp.bfloat16)
        return hidden_grad, slot_grad, partial_grad

    def one_group(total, inputs):
        dy_group, gate_group, route_group, hidden_group = inputs
        place = jax.vmap(lambda route: slot_table(route, EXPERTS, CAP))(route_group).astype(jnp.float32)
        sent = jnp.einsum("stc,std->scd", place, dy_group.astype(jnp.float32)).astype(jnp.bfloat16)
        sent = sent.reshape(N_EXPERT, EXPERTS, CAP, D).transpose(1, 0, 2, 3).reshape(EXPERTS, SLOTS, D)
        gate_sent = jnp.einsum("stc,st->sc", place, gate_group.astype(jnp.float32)).astype(jnp.bfloat16)
        gate_sent = gate_sent.reshape(N_EXPERT, EXPERTS, CAP).transpose(1, 0, 2).reshape(EXPERTS, SLOTS)
        hidden_grad, slot_grad, partial_grad = lax.map(per_expert, (sent, gate_sent, hidden_group, down_weight))
        back = slot_grad.reshape(EXPERTS, N_EXPERT, CAP).transpose(1, 0, 2).reshape(N_EXPERT, EXPERTS * CAP)
        token_grad = jnp.einsum("stc,sc->st", place, back, precision=lax.Precision.HIGHEST)
        return total + partial_grad.astype(jnp.float32), (hidden_grad, token_grad.reshape(N_EXPERT * TOK_DEV))

    start = jnp.zeros((EXPERTS, H, D), jnp.float32)
    total, (hidden_all, gate_all_grad) = lax.scan(one_group, start, (dy_all, gate_all, route_all, saved_hidden))
    return hidden_all, total, gate_all_grad.reshape(TOKENS)
```

```python
import functools

import jax
import jax.numpy as jnp
from jax import lax
from jax.experimental import pallas as pl
from jax.experimental.pallas import tpu as pltpu
from jax.sharding import PartitionSpec as P

MESH = pl.DeviceIdType.MESH
LANES = 128
MAIN = 32
EXTRA = 2
BF = jnp.bfloat16
F32 = jnp.float32


def slot_table(route, experts, cap):
    onehot = (route[:, None] == jnp.arange(experts, dtype=jnp.int32)[None, :]).astype(jnp.int32)
    before = jnp.cumsum(onehot, axis=0) - onehot
    rank = jnp.sum(before * onehot, axis=1)
    slot = route * cap + rank
    return slot[:, None] == jnp.arange(experts * cap, dtype=jnp.int32)[None, :]


def scaled_rows(rows, exponent):
    count, width = rows.shape
    blocks = exponent.shape[1]
    factor = 1.0 / jnp.left_shift(jnp.ones_like(exponent), exponent).astype(jnp.float32)
    scaled = rows.astype(jnp.float32).reshape(count, blocks, width // blocks) * factor[:, :, None]
    return scaled.reshape(count, width).astype(jnp.bfloat16)


def local_general(grad_rows, grad_exponent, gate, routing, saved_hidden, down_weight):
    experts = lax.axis_size("expert")
    slots = saved_hidden.shape[2]
    cap = slots // experts
    width = grad_rows.shape[1]
    dy_local = scaled_rows(grad_rows, grad_exponent)
    place = slot_table(routing[:, 0], experts, cap)
    place_low = place.astype(jnp.bfloat16)
    sent = lax.dot_general(
        place_low, dy_local, (((0,), (0,)), ((), ())), preferred_element_type=jnp.float32
    )
    sent = sent.astype(jnp.bfloat16).reshape(experts, cap, width)
    gate_sent = jnp.dot(gate, place_low, preferred_element_type=jnp.float32)
    gate_sent = gate_sent.astype(jnp.bfloat16).reshape(experts, cap)
    arrived, arrived_gate = (
        lax.all_to_all(sent, "expert", split_axis=0, concat_axis=0, tiled=True),
        lax.all_to_all(gate_sent, "expert", split_axis=0, concat_axis=0, tiled=True),
    )
    rows = arrived.reshape(slots, width)
    gates = arrived_gate.reshape(slots).astype(jnp.float32)
    weight = down_weight[0]
    hidden = saved_hidden[0, 0]
    raw = lax.dot_general(
        rows, weight, (((1,), (1,)), ((), ())), preferred_element_type=jnp.float32
    )
    hidden_grad = (gates[:, None] * raw).astype(jnp.bfloat16)
    slot_grad = jnp.sum(hidden.astype(jnp.float32) * raw, axis=1)
    back = lax.all_to_all(
        slot_grad.reshape(experts, cap), "expert", split_axis=0, concat_axis=0, tiled=True
    )
    gate_grad = jnp.dot(
        place.astype(jnp.float32), back.reshape(slots), precision=lax.Precision.HIGHEST
    )
    weighted = (gates[:, None] * rows.astype(jnp.float32)).astype(jnp.bfloat16)
    weight_grad = lax.psum_scatter(
        lax.dot_general(
            hidden, weighted, (((0,), (0,)), ((), ())), preferred_element_type=jnp.float32
        ).astype(jnp.bfloat16),
        "dp",
        scatter_dimension=0,
        tiled=True,
    ).astype(jnp.float32)
    return (hidden_grad[None, None], weight_grad[None], gate_grad)


def iota(shape, axis):
    return lax.broadcasted_iota(jnp.int32, shape, axis)


def dot(a, b, dims=((1,), (0,)), precision=None):
    return lax.dot_general(a, b, (dims, ((), ())), preferred_element_type=F32, precision=precision)


def slot_of(i):
    main = i < 4 * MAIN
    j = i - 4 * MAIN
    source = jnp.where(main, i >> 5, j >> 1)
    rank = jnp.where(main, i & 31, MAIN + (j & 1))
    return source, rank


def pack_match(a, b):
    q = a & 15
    r = (q >= 7).astype(jnp.int32)
    return (q < 14) & (b == (q - 7 * r) * 16 + (a >> 4) * 2 + r)


def kernel(
    cap,
    chunks,
    rows_ref,
    exp_ref,
    gate_ref,
    route_ref,
    hidden_ref,
    weight_ref,
    hidden_grad_ref,
    weight_grad_ref,
    gate_grad_ref,
    dy,
    sent,
    sent_pack,
    rows,
    pack,
    gath,
    hblk,
    hg,
    wbuf,
    rs_send,
    rs_recv,
    wg,
    back_send,
    back_recv,
    pack_s,
    pack_r,
    z_s,
    z_r,
    h_s,
    h_r,
    core_s,
    core_r,
    nb_s,
    nb_r,
    relay_s,
    relay_r,
    rs_s,
    rs_r,
    back_s,
    back_r,
    w_sem,
    out_sem,
):
    d = lax.axis_index("dp")
    me = lax.axis_index("expert")
    c = lax.rem(d, 2)
    x = lax.rem(lax.div(d, 2), 2)
    y = lax.div(d, 4)

    def dp_at(yy, xx, cc):
        return (yy * 2 + xx) * 2 + cc

    width = rows_ref.shape[1]
    wide = width // chunks
    blocks = wide // LANES
    total = 4 * MAIN + 16
    other = dp_at(y, x, 1 - c)
    near = (dp_at(y, 1 - x, c), dp_at(1 - y, x, c))
    near_other = (dp_at(y, 1 - x, 1 - c), dp_at(1 - y, x, 1 - c))
    peers_z = [lax.rem(me + o, 4) for o in (1, 2, 3)]

    load = pltpu.make_async_copy(weight_ref, wbuf, w_sem)
    load.start()

    barrier = pltpu.get_barrier_semaphore()
    for e in peers_z:
        pl.semaphore_signal(barrier, inc=1, device_id=(d, e), device_id_type=MESH)
    for p in (other,) + near + near_other:
        pl.semaphore_signal(barrier, inc=1, device_id=(p, me), device_id_type=MESH)

    def remote(src, dst, s, r, p, e):
        return pltpu.make_async_remote_copy(
            src_ref=src, dst_ref=dst, send_sem=s, recv_sem=r, device_id=(p, e), device_id_type=MESH
        )

    route = route_ref[...]
    onehot = iota((16, LANES), 0) == route
    onehot_low = onehot.astype(F32).astype(BF)
    earlier = (iota((LANES, LANES), 0) < iota((LANES, LANES), 1)).astype(F32).astype(BF)
    before = dot(onehot_low, earlier)
    rank = jnp.sum(jnp.where(onehot, before, 0.0), axis=0, keepdims=True).astype(jnp.int32)
    main_at = jnp.where(rank < MAIN, route * MAIN + rank, -1)
    extra_at = jnp.where(rank < MAIN, -1, route * EXTRA + rank - MAIN)
    place = (iota((LANES, LANES), 0) == main_at).astype(F32).astype(BF)
    place_extra = (iota((16, LANES), 0) == extra_at).astype(F32).astype(BF)
    rank_is = (iota((LANES, LANES), 0) == rank).astype(F32)
    gate_slots = dot(
        jnp.where(onehot, gate_ref[...], 0.0).astype(BF), rank_is.astype(BF), ((1,), (1,))
    ).astype(BF)

    factor = 1.0 / lax.shift_left(jnp.ones(exp_ref.shape, jnp.int32), exp_ref[...]).astype(F32)
    for b in range(width // LANES):
        columns = pl.ds(b * LANES, LANES)
        dy[:, columns] = (rows_ref[:, columns].astype(F32) * factor[:, b : b + 1]).astype(BF)
    packing = pack_match(iota((64, 16 * blocks), 0), iota((64, 16 * blocks), 1))
    packing = packing.astype(F32).astype(BF)
    at = iota((64, 16), 0)
    gate_row = (((at & 15) == 14) & ((at >> 4) == iota((64, 16), 1))).astype(F32).astype(BF)
    for k in range(chunks):
        extra = dot(place_extra, dy[:, k * wide : (k + 1) * wide]).astype(BF)
        stacked = jnp.concatenate(
            [extra[:, b * LANES : (b + 1) * LANES] for b in range(blocks)], axis=0
        )
        tile = dot(packing, stacked)
        if k == 0:
            tile = tile + dot(gate_row, gate_slots)
        sent_pack[:, k * 16 : (k + 1) * 16, :] = tile.astype(BF).reshape(4, 16, LANES)
    pl.semaphore_wait(barrier, 8)
    sends = []
    pack_copies = []
    for i, e in enumerate(peers_z):
        copy = remote(sent_pack.at[e], pack.at[me], pack_s.at[i], pack_r.at[i], d, e)
        copy.start()
        pack_copies.append(copy)
    pack[me] = sent_pack[me]
    z_copies = []
    own_rows = pl.ds(pl.multiple_of(me * MAIN, MAIN), MAIN)
    for k in range(chunks):
        sent[k] = dot(place, dy[:, k * wide : (k + 1) * wide]).astype(BF)
        group = []
        for i, e in enumerate(peers_z):
            copy = remote(
                sent.at[k, pl.ds(pl.multiple_of(e * MAIN, MAIN), MAIN)],
                rows.at[k, own_rows],
                z_s.at[k, i],
                z_r.at[k, i],
                d,
                e,
            )
            copy.start()
            group.append(copy)
        rows[k, own_rows, :] = sent[k, own_rows, :]
        z_copies.append(group)

    slots = hidden_ref.shape[0]
    source, in_source = slot_of(iota((total, slots), 0))
    order = ((source < 4) & (iota((total, slots), 1) == source * cap + in_source))
    hidden = dot(order.astype(F32).astype(BF), hidden_ref[...]).astype(BF)
    for b in range(8):
        hblk[b] = hidden[:, b * LANES : (b + 1) * LANES]
    h_copies = []
    for t in range(2):
        for j, p in ((1, other), (2, near[t]), (3, near_other[t])):
            pc = lax.rem(p, 2)
            px = lax.rem(lax.div(p, 2), 2)
            py = lax.div(p, 4)
            partner = dp_at(1 - py, px, pc) if t == 0 else dp_at(py, 1 - px, pc)
            for b, block in enumerate((partner, p)):
                copy = remote(
                    hblk.at[block], hg.at[t, b, j], h_s.at[t, b, j], h_r.at[t, b, j], p, me
                )
                copy.start()
                h_copies.append(copy)
        for b, block in enumerate((near[1 - t], d)):
            hg[t, b, 0] = hblk[block]

    for copy in pack_copies:
        copy.wait_recv()
    wide_at = iota((total, 64), 0)
    source, _ = slot_of(wide_at)
    pick = ((source < 4) & (iota((total, 64), 1) == source * 16 + 14)).astype(F32).astype(BF)
    spread = dot(pick, pack[:, 0:16, :].reshape(64, LANES))
    source, in_source = slot_of(iota((total, LANES), 0))
    lane_is = (source < 4) & (iota((total, LANES), 1) == in_source)
    gates = jnp.sum(jnp.where(lane_is, spread, 0.0), axis=1, keepdims=True)
    unpacking = pack_match(iota((16 * blocks, 64), 1), iota((16 * blocks, 64), 0))
    unpacking = unpacking.astype(F32).astype(BF)

    core_copies, nb_copies, relay_copies, rs_copies, outs = [], [], [], [], []
    raw = None

    def own_chunk(k):
        t = k % 2
        spread_rows = dot(unpacking, pack[:, k * 16 : (k + 1) * 16, :].reshape(64, LANES))
        for b in range(blocks):
            rows[k, 4 * MAIN :, b * LANES : (b + 1) * LANES] = spread_rows[
                b * 16 : (b + 1) * 16
            ].astype(BF)
        for copy in z_copies[k]:
            copy.wait_recv()
        gath[k, 0] = (gates * rows[k].astype(F32)).astype(BF)
        copy = remote(gath.at[k, 0], gath.at[k, 2], nb_s.at[k], nb_r.at[k], near[t], me)
        copy.start()
        nb_copies.append(copy)
        copy = remote(gath.at[k, 0], gath.at[k, 1], core_s.at[k], core_r.at[k], other, me)
        copy.start()
        core_copies.append(copy)

    def relay_chunk(k):
        nb_copies[k].wait_recv()
        copy = remote(gath.at[k, 2], gath.at[k, 3], relay_s.at[k], relay_r.at[k], other, me)
        copy.start()
        relay_copies.append(copy)

    def partial_chunk(k):
        t = k % 2
        core_copies[k].wait_recv()
        relay_copies[k].wait_recv()
        gathered = gath[k].reshape(4 * total, wide)
        rs_send[k] = dot(hg[t, 0].reshape(4 * total, LANES), gathered, ((0,), (0,))).astype(BF)
        copy = remote(rs_send.at[k], rs_recv.at[k], rs_s.at[k], rs_r.at[k], near[1 - t], me)
        copy.start()
        rs_copies.append(copy)
        wg[k] = dot(hg[t, 1].reshape(4 * total, LANES), gathered, ((0,), (0,)))

    for step in range(chunks + 1):
        if step < chunks:
            own_chunk(step)
        if step >= 1:
            relay_chunk(step - 1)
        if step < chunks:
            if step == 0:
                load.wait()
            term = dot(rows[step], wbuf[:, step * wide : (step + 1) * wide], ((1,), (1,)))
            raw = term if raw is None else raw + term
        if step == 1:
            for copy in h_copies:
                copy.wait_recv()
        if step == chunks - 1:
            slot_grad = jnp.sum(hidden.astype(F32) * raw, axis=1, keepdims=True)
            in_lane = jnp.where(lane_is, slot_grad, 0.0)
            tail = in_lane[4 * MAIN :]
            tail_at = iota(tail.shape, 0) >> 1
            for s in range(4):
                line = jnp.sum(in_lane[s * MAIN : (s + 1) * MAIN], axis=0, keepdims=True)
                line = line + jnp.sum(jnp.where(tail_at == s, tail, 0.0), axis=0, keepdims=True)
                back_send[s] = jnp.broadcast_to(line, (8, LANES))
            back_copies = []
            for i, e in enumerate(peers_z):
                copy = remote(back_send.at[e], back_recv.at[me], back_s.at[i], back_r.at[i], d, e)
                copy.start()
                back_copies.append(copy)
            back_recv[me] = back_send[me]
        if step >= 1:
            partial_chunk(step - 1)

    scaled = (gates * raw).astype(BF)
    source, in_source = slot_of(iota((slots, total), 1))
    order = ((source < 4) & (iota((slots, total), 0) == source * cap + in_source))
    hidden_grad_ref[...] = dot(order.astype(F32).astype(BF), scaled).astype(BF)

    for copy in back_copies:
        copy.wait_recv()
    taken = dot(
        back_recv[...].reshape(4 * 8, LANES), rank_is, precision=lax.Precision.HIGHEST
    )
    answer = jnp.zeros((1, LANES), F32)
    for e in range(4):
        answer = answer + jnp.where(route == e, taken[e * 8 : e * 8 + 1], 0.0)
    gate_grad_ref[...] = answer

    for k in range(chunks):
        rs_copies[k].wait_recv()
        wg[k] = wg[k] + rs_recv[k].astype(F32)
        copy = pltpu.make_async_copy(
            wg.at[k], weight_grad_ref.at[:, pl.ds(k * wide, wide)], out_sem.at[k]
        )
        copy.start()
        outs.append(copy)
    for copy in (
        pack_copies
        + [one for group in z_copies for one in group]
        + h_copies
        + core_copies
        + nb_copies
        + relay_copies
        + rs_copies
        + back_copies
    ):
        copy.wait_send()
    for copy in outs:
        copy.wait()


def local_fused(chunks, grad_rows, grad_exponent, gate, routing, saved_hidden, down_weight):
    tokens, width = grad_rows.shape
    slots, units = saved_hidden.shape[2:]
    cap = slots // 4
    wide = width // chunks
    total = 4 * MAIN + 16
    dma = pltpu.SemaphoreType.DMA
    vmem = pl.BlockSpec(memory_space=pltpu.VMEM)
    anywhere = pl.BlockSpec(memory_space=pl.ANY)
    hidden_grad, weight_grad, gate_grad = pl.pallas_call(
        functools.partial(kernel, cap, chunks),
        out_shape=(
            jax.ShapeDtypeStruct((slots, units), BF),
            jax.ShapeDtypeStruct((units // 8, width), F32),
            jax.ShapeDtypeStruct((1, tokens), F32),
        ),
        in_specs=[vmem] * 5 + [anywhere],
        out_specs=(vmem, anywhere, vmem),
        scratch_shapes=[
            pltpu.VMEM((tokens, width), BF),
            pltpu.VMEM((chunks, 4 * MAIN, wide), BF),
            pltpu.VMEM((4, 16 * chunks, LANES), BF),
            pltpu.VMEM((chunks, total, wide), BF),
            pltpu.VMEM((4, 16 * chunks, LANES), BF),
            pltpu.VMEM((chunks, 4, total, wide), BF),
            pltpu.VMEM((8, total, LANES), BF),
            pltpu.VMEM((2, 2, 4, total, LANES), BF),
            pltpu.VMEM((units, width), BF),
            pltpu.VMEM((chunks, LANES, wide), BF),
            pltpu.VMEM((chunks, LANES, wide), BF),
            pltpu.VMEM((chunks, LANES, wide), F32),
            pltpu.VMEM((4, 8, LANES), F32),
            pltpu.VMEM((4, 8, LANES), F32),
            dma((3,)),
            dma((3,)),
            dma((chunks, 3)),
            dma((chunks, 3)),
            dma((2, 2, 4)),
            dma((2, 2, 4)),
            dma((chunks,)),
            dma((chunks,)),
            dma((chunks,)),
            dma((chunks,)),
            dma((chunks,)),
            dma((chunks,)),
            dma((chunks,)),
            dma((chunks,)),
            dma((3,)),
            dma((3,)),
            dma,
            dma((chunks,)),
        ],
        compiler_params=pltpu.CompilerParams(
            collective_id=0, has_side_effects=True, vmem_limit_bytes=56 * 1024 * 1024
        ),
        cost_estimate=pl.CostEstimate(
            flops=4 * slots * units * width, bytes_accessed=2 * units * width, transcendentals=0
        ),
    )(
        grad_rows,
        grad_exponent,
        gate.astype(F32).reshape(1, tokens),
        routing.reshape(1, tokens),
        saved_hidden.reshape(slots, units),
        down_weight.reshape(units, width),
    )
    return (hidden_grad[None, None], weight_grad[None], gate_grad.reshape(tokens))


def solution(mesh):
    in_specs = (
        P(("dp", "expert"), None),
        P(("dp", "expert"), None),
        P(("dp", "expert")),
        P(("dp", "expert"), None),
        P("dp", "expert", None, None),
        P("expert", None, None),
    )
    out_specs = (P("dp", "expert", None, None), P("expert", "dp", None), P(("dp", "expert")))

    def local(grad_rows, grad_exponent, gate, routing, saved_hidden, down_weight):
        args = (grad_rows, grad_exponent, gate, routing, saved_hidden, down_weight)
        tokens, width = grad_rows.shape
        slots, units = saved_hidden.shape[2:]
        fits = mesh.shape["dp"] == 8 and mesh.shape["expert"] == 4 and tokens == LANES
        fits = fits and slots == 4 * (MAIN + EXTRA) and units == 8 * LANES
        if fits and width == 4 * 7 * LANES:
            return local_fused(4, *args)
        return local_general(*args)

    return jax.shard_map(local, mesh=mesh, in_specs=in_specs, out_specs=out_specs, check_vma=False)
```

```python
import functools

import jax
import jax.numpy as jnp
from jax import lax
from jax.experimental import pallas as pl
from jax.experimental.pallas import tpu as pltpu
from jax.sharding import PartitionSpec as P

MESH = pl.DeviceIdType.MESH
LANES = 128
MAIN = 32
EXTRA = 2
GATE_ROW = 56
BF = jnp.bfloat16
F32 = jnp.float32


def slot_table(route, experts, cap):
    onehot = (route[:, None] == jnp.arange(experts, dtype=jnp.int32)[None, :]).astype(jnp.int32)
    before = jnp.cumsum(onehot, axis=0) - onehot
    rank = jnp.sum(before * onehot, axis=1)
    slot = route * cap + rank
    return slot[:, None] == jnp.arange(experts * cap, dtype=jnp.int32)[None, :]


def scaled_rows(rows, exponent):
    count, width = rows.shape
    blocks = exponent.shape[1]
    factor = 1.0 / jnp.left_shift(jnp.ones_like(exponent), exponent).astype(jnp.float32)
    scaled = rows.astype(jnp.float32).reshape(count, blocks, width // blocks) * factor[:, :, None]
    return scaled.reshape(count, width).astype(jnp.bfloat16)


def local_general(grad_rows, grad_exponent, gate, routing, saved_hidden, down_weight):
    experts = lax.axis_size("expert")
    slots = saved_hidden.shape[2]
    cap = slots // experts
    width = grad_rows.shape[1]
    dy_local = scaled_rows(grad_rows, grad_exponent)
    place = slot_table(routing[:, 0], experts, cap)
    place_low = place.astype(jnp.bfloat16)
    sent = lax.dot_general(
        place_low, dy_local, (((0,), (0,)), ((), ())), preferred_element_type=jnp.float32
    )
    sent = sent.astype(jnp.bfloat16).reshape(experts, cap, width)
    gate_sent = jnp.dot(gate, place_low, preferred_element_type=jnp.float32)
    gate_sent = gate_sent.astype(jnp.bfloat16).reshape(experts, cap)
    arrived, arrived_gate = (
        lax.all_to_all(sent, "expert", split_axis=0, concat_axis=0, tiled=True),
        lax.all_to_all(gate_sent, "expert", split_axis=0, concat_axis=0, tiled=True),
    )
    rows = arrived.reshape(slots, width)
    gates = arrived_gate.reshape(slots).astype(jnp.float32)
    weight = down_weight[0]
    hidden = saved_hidden[0, 0]
    raw = lax.dot_general(
        rows, weight, (((1,), (1,)), ((), ())), preferred_element_type=jnp.float32
    )
    hidden_grad = (gates[:, None] * raw).astype(jnp.bfloat16)
    slot_grad = jnp.sum(hidden.astype(jnp.float32) * raw, axis=1)
    back = lax.all_to_all(
        slot_grad.reshape(experts, cap), "expert", split_axis=0, concat_axis=0, tiled=True
    )
    gate_grad = jnp.dot(
        place.astype(jnp.float32), back.reshape(slots), precision=lax.Precision.HIGHEST
    )
    weighted = (gates[:, None] * rows.astype(jnp.float32)).astype(jnp.bfloat16)
    weight_grad = lax.psum_scatter(
        lax.dot_general(
            hidden, weighted, (((0,), (0,)), ((), ())), preferred_element_type=jnp.float32
        ).astype(jnp.bfloat16),
        "dp",
        scatter_dimension=0,
        tiled=True,
    ).astype(jnp.float32)
    return (hidden_grad[None, None], weight_grad[None], gate_grad)


def iota(shape, axis):
    return lax.broadcasted_iota(jnp.int32, shape, axis)


def dot(a, b, dims=((1,), (0,)), precision=None):
    return lax.dot_general(a, b, (dims, ((), ())), preferred_element_type=F32, precision=precision)


def slot_of(i):
    main = i < 4 * MAIN
    j = i - 4 * MAIN
    source = jnp.where(main, i >> 5, j >> 1)
    rank = jnp.where(main, i & 31, MAIN + (j & 1))
    return source, rank


def pack_match(blocks, a, b):
    q = a & 63
    r = (q >= blocks).astype(jnp.int32)
    return (q < 2 * blocks) & (b == (q - blocks * r) * 16 + (a >> 6) * 2 + r)


def kernel(
    cap,
    chunks,
    ahead,
    rows_ref,
    exp_ref,
    gate_ref,
    route_ref,
    hidden_ref,
    weight_ref,
    hidden_grad_ref,
    weight_grad_ref,
    gate_grad_ref,
    dy,
    sent,
    sent_pack,
    rows,
    pack,
    gath,
    hblk,
    hg,
    wbuf,
    rs_send,
    rs_recv,
    wg,
    back_send,
    back_recv,
    pack_s,
    pack_r,
    z_s,
    z_r,
    h_s,
    h_r,
    core_s,
    core_r,
    nb_s,
    nb_r,
    relay_s,
    relay_r,
    rs_s,
    rs_r,
    back_s,
    back_r,
    w_sem,
):
    d = lax.axis_index("dp")
    me = lax.axis_index("expert")
    c = lax.rem(d, 2)
    x = lax.rem(lax.div(d, 2), 2)
    y = lax.div(d, 4)

    def dp_at(yy, xx, cc):
        return (yy * 2 + xx) * 2 + cc

    width = rows_ref.shape[1]
    wide = width // chunks
    blocks = wide // LANES
    half = wide // 2
    all_blocks = width // LANES
    total = 4 * MAIN + 16
    other = dp_at(y, x, 1 - c)
    near = (dp_at(y, 1 - x, c), dp_at(1 - y, x, c))
    near_other = (dp_at(y, 1 - x, 1 - c), dp_at(1 - y, x, 1 - c))
    peers_z = [lax.rem(me + o, 4) for o in (1, 2, 3)]

    load = pltpu.make_async_copy(weight_ref, wbuf, w_sem)
    load.start()

    barrier = pltpu.get_barrier_semaphore()
    for e in peers_z:
        pl.semaphore_signal(barrier, inc=1, device_id=(d, e), device_id_type=MESH)
    for p in (other,) + near + near_other:
        pl.semaphore_signal(barrier, inc=1, device_id=(p, me), device_id_type=MESH)

    def remote(src, dst, s, r, p, e):
        return pltpu.make_async_remote_copy(
            src_ref=src, dst_ref=dst, send_sem=s, recv_sem=r, device_id=(p, e), device_id_type=MESH
        )

    route = route_ref[...]
    onehot = iota((16, LANES), 0) == route
    onehot_low = onehot.astype(F32).astype(BF)
    earlier = (iota((LANES, LANES), 0) < iota((LANES, LANES), 1)).astype(F32).astype(BF)
    before = dot(onehot_low, earlier)
    rank = jnp.sum(jnp.where(onehot, before, 0.0), axis=0, keepdims=True).astype(jnp.int32)
    main_at = jnp.where(rank < MAIN, route * MAIN + rank, -1)
    extra_at = jnp.where(rank < MAIN, -1, route * EXTRA + rank - MAIN)
    place = (iota((LANES, LANES), 0) == main_at).astype(F32).astype(BF)
    place_extra = (iota((16, LANES), 0) == extra_at).astype(F32).astype(BF)
    rank_is = (iota((LANES, LANES), 0) == rank).astype(F32)
    gate_slots = dot(
        jnp.where(onehot, gate_ref[...], 0.0).astype(BF), rank_is.astype(BF), ((1,), (1,))
    ).astype(BF)

    factor = 1.0 / lax.shift_left(jnp.ones(exp_ref.shape, jnp.int32), exp_ref[...]).astype(F32)
    factor = jnp.concatenate([factor, jnp.zeros((32 - all_blocks, LANES), F32)], axis=0).T
    for b in range(all_blocks):
        columns = pl.ds(b * LANES, LANES)
        dy[:, columns] = (rows_ref[:, columns].astype(F32) * factor[:, b : b + 1]).astype(BF)
    extra = dot(place_extra, dy[...]).astype(BF)
    stacked = jnp.concatenate(
        [extra[:, b * LANES : (b + 1) * LANES] for b in range(all_blocks)], axis=0
    )
    at = (4 * 64, 16 * all_blocks)
    packing = pack_match(all_blocks, iota(at, 0), iota(at, 1)).astype(F32).astype(BF)
    at = iota((4 * 64, 16), 0)
    gate_row = (((at & 63) == GATE_ROW) & ((at >> 6) == iota((4 * 64, 16), 1))).astype(F32)
    tile = dot(packing, stacked) + dot(gate_row.astype(BF), gate_slots)
    sent_pack[...] = tile.astype(BF).reshape(4, 64, LANES)
    own_rows = pl.ds(pl.multiple_of(me * MAIN, MAIN), MAIN)
    z_copies = []

    def dispatch(k):
        sent[k] = dot(place, dy[:, k * wide : (k + 1) * wide]).astype(BF)
        if k == 0:
            pl.semaphore_wait(barrier, 8)
            for i, e in enumerate(peers_z):
                copy = remote(sent_pack.at[e], pack.at[me], pack_s.at[i], pack_r.at[i], d, e)
                copy.start()
                pack_copies.append(copy)
            pack[me] = sent_pack[me]
        group = []
        for i, e in enumerate(peers_z):
            copy = remote(
                sent.at[k, pl.ds(pl.multiple_of(e * MAIN, MAIN), MAIN)],
                rows.at[k, own_rows],
                z_s.at[k, i],
                z_r.at[k, i],
                d,
                e,
            )
            copy.start()
            group.append(copy)
        rows[k, own_rows, :] = sent[k, own_rows, :]
        z_copies.append(group)

    pack_copies = []
    for k in range(ahead):
        dispatch(k)

    slots = hidden_ref.shape[0]
    source, in_source = slot_of(iota((total, slots), 0))
    order = ((source < 4) & (iota((total, slots), 1) == source * cap + in_source))
    hidden = dot(order.astype(F32).astype(BF), hidden_ref[...]).astype(BF)
    for b in range(8):
        hblk[b] = hidden[:, b * LANES : (b + 1) * LANES]
    h_copies = []
    for t in range(2):
        for j, p in ((1, other), (2, near[t]), (3, near_other[t])):
            pc = lax.rem(p, 2)
            px = lax.rem(lax.div(p, 2), 2)
            py = lax.div(p, 4)
            partner = dp_at(1 - py, px, pc) if t == 0 else dp_at(py, 1 - px, pc)
            for b, block in enumerate((partner, p)):
                copy = remote(
                    hblk.at[block], hg.at[t, b, j], h_s.at[t, b, j], h_r.at[t, b, j], p, me
                )
                copy.start()
                h_copies.append(copy)
        for b, block in enumerate((near[1 - t], d)):
            hg[t, b, 0] = hblk[block]

    for copy in pack_copies:
        copy.wait_recv()
    at = (total, 4 * 64)
    source, _ = slot_of(iota(at, 0))
    pick = ((source < 4) & (iota(at, 1) == source * 64 + GATE_ROW)).astype(F32).astype(BF)
    spread = dot(pick, pack[...].reshape(4 * 64, LANES))
    source, in_source = slot_of(iota((total, LANES), 0))
    lane_is = (source < 4) & (iota((total, LANES), 1) == in_source)
    gates = jnp.sum(jnp.where(lane_is, spread, 0.0), axis=1, keepdims=True)

    core_copies, nb_copies, relay_copies, rs_copies = [], [], [], []
    raw = None

    def own_chunk(k):
        at = (16 * blocks, 4 * 64)
        unpacking = pack_match(all_blocks, iota(at, 1), iota(at, 0) + k * 16 * blocks)
        spread_rows = dot(unpacking.astype(F32).astype(BF), pack[...].reshape(4 * 64, LANES))
        for b in range(blocks):
            rows[k, 4 * MAIN :, b * LANES : (b + 1) * LANES] = spread_rows[
                b * 16 : (b + 1) * 16
            ].astype(BF)
        for copy in z_copies[k]:
            copy.wait_recv()
        if k + ahead < chunks:
            dispatch(k + ahead)
        pair = []
        for t in range(2):
            part = rows[k, :, t * half : (t + 1) * half].astype(F32)
            gath[k, 0, t] = (gates * part).astype(BF)
            copy = remote(
                gath.at[k, 0, t], gath.at[k, 2, t], nb_s.at[k, t], nb_r.at[k, t], near[t], me
            )
            copy.start()
            pair.append(copy)
        nb_copies.append(pair)
        copy = remote(gath.at[k, 0], gath.at[k, 1], core_s.at[k], core_r.at[k], other, me)
        copy.start()
        core_copies.append(copy)

    def relay_chunk(k):
        for copy in nb_copies[k]:
            copy.wait_recv()
        copy = remote(gath.at[k, 2], gath.at[k, 3], relay_s.at[k], relay_r.at[k], other, me)
        copy.start()
        relay_copies.append(copy)

    def partial_chunk(k):
        core_copies[k].wait_recv()
        relay_copies[k].wait_recv()
        pair = []
        for t in range(2):
            gathered = gath[k, :, t].reshape(4 * total, half)
            away = dot(hg[t, 0].reshape(4 * total, LANES), gathered, ((0,), (0,)))
            rs_send[k, t] = away.astype(BF)
            copy = remote(
                rs_send.at[k, t], rs_recv.at[k, t], rs_s.at[k, t], rs_r.at[k, t], near[1 - t], me
            )
            copy.start()
            pair.append(copy)
        rs_copies.append(pair)
        for t in range(2):
            gathered = gath[k, :, t].reshape(4 * total, half)
            wg[k, :, t * half : (t + 1) * half] = dot(
                hg[t, 1].reshape(4 * total, LANES), gathered, ((0,), (0,))
            )

    for step in range(chunks + 1):
        if step < chunks:
            own_chunk(step)
        if step >= 1:
            relay_chunk(step - 1)
        if step < chunks:
            if step == 0:
                load.wait()
            term = dot(rows[step], wbuf[:, step * wide : (step + 1) * wide], ((1,), (1,)))
            raw = term if raw is None else raw + term
        if step == 1:
            for copy in h_copies:
                copy.wait_recv()
        if step == chunks - 1:
            slot_grad = jnp.sum(hidden.astype(F32) * raw, axis=1, keepdims=True)
            in_lane = jnp.where(lane_is, slot_grad, 0.0)
            tail = in_lane[4 * MAIN :]
            tail_at = iota(tail.shape, 0) >> 1
            for s in range(4):
                line = jnp.sum(in_lane[s * MAIN : (s + 1) * MAIN], axis=0, keepdims=True)
                line = line + jnp.sum(jnp.where(tail_at == s, tail, 0.0), axis=0, keepdims=True)
                back_send[s] = jnp.broadcast_to(line, (8, LANES))
            back_copies = []
            for i, e in enumerate(peers_z):
                copy = remote(back_send.at[e], back_recv.at[me], back_s.at[i], back_r.at[i], d, e)
                copy.start()
                back_copies.append(copy)
            back_recv[me] = back_send[me]
        if step >= 1:
            partial_chunk(step - 1)

    scaled = (gates * raw).astype(BF)
    source, in_source = slot_of(iota((slots, total), 1))
    order = ((source < 4) & (iota((slots, total), 0) == source * cap + in_source))
    hidden_grad_ref[...] = dot(order.astype(F32).astype(BF), scaled).astype(BF)

    for copy in back_copies:
        copy.wait_recv()
    taken = dot(
        back_recv[...].reshape(4 * 8, LANES), rank_is, precision=lax.Precision.HIGHEST
    )
    answer = jnp.zeros((1, LANES), F32)
    for e in range(4):
        answer = answer + jnp.where(route == e, taken[e * 8 : e * 8 + 1], 0.0)
    gate_grad_ref[...] = answer

    for k in range(chunks):
        for t in range(2):
            rs_copies[k][t].wait_recv()
            columns = pl.ds(t * half, half)
            target = pl.ds(k * wide + t * half, half)
            weight_grad_ref[:, target] = wg[k, :, columns] + rs_recv[k, t].astype(F32)
    for copy in (
        pack_copies
        + [one for group in z_copies for one in group]
        + h_copies
        + core_copies
        + [one for pair in nb_copies for one in pair]
        + relay_copies
        + [one for pair in rs_copies for one in pair]
        + back_copies
    ):
        copy.wait_send()


PIECES = 8


def finish_kernel(*refs):
    sources, targets, sem = refs[:3], refs[3:6], refs[6]
    copies = []
    step = sources[1].shape[0] // PIECES
    for i in range(PIECES):
        at = pl.ds(i * step, step)
        copies.append(
            pltpu.make_async_copy(sources[1].at[at], targets[1].at[at], sem.at[i])
        )
    for i, j in ((0, PIECES), (2, PIECES + 1)):
        copies.append(pltpu.make_async_copy(sources[i], targets[i], sem.at[j]))
    for copy in copies:
        copy.start()
    for copy in copies:
        copy.wait()


def finish(*arrays):
    anywhere = pl.BlockSpec(memory_space=pl.ANY)
    return pl.pallas_call(
        finish_kernel,
        out_shape=tuple(jax.ShapeDtypeStruct(a.shape, a.dtype) for a in arrays),
        in_specs=[pl.BlockSpec(memory_space=pltpu.VMEM)] * 3,
        out_specs=(anywhere,) * 3,
        scratch_shapes=[pltpu.SemaphoreType.DMA((PIECES + 2,))],
        compiler_params=pltpu.CompilerParams(vmem_limit_bytes=16 * 1024 * 1024),
    )(*arrays)


def local_fused(chunks, ahead, grad_rows, grad_exponent, gate, routing, saved_hidden, down_weight):
    tokens, width = grad_rows.shape
    slots, units = saved_hidden.shape[2:]
    cap = slots // 4
    wide = width // chunks
    total = 4 * MAIN + 16
    dma = pltpu.SemaphoreType.DMA
    vmem = pl.BlockSpec(memory_space=pltpu.VMEM)
    anywhere = pl.BlockSpec(memory_space=pl.ANY)
    hidden_grad, weight_grad, gate_grad = pl.pallas_call(
        functools.partial(kernel, cap, chunks, ahead),
        out_shape=(
            pltpu.VMEM((slots, units), BF),
            pltpu.VMEM((units // 8, width), F32),
            pltpu.VMEM((1, tokens), F32),
        ),
        in_specs=[vmem] * 5 + [anywhere],
        out_specs=(vmem, vmem, vmem),
        scratch_shapes=[
            pltpu.VMEM((tokens, width), BF),
            pltpu.VMEM((chunks, 4 * MAIN, wide), BF),
            pltpu.VMEM((4, 64, LANES), BF),
            pltpu.VMEM((chunks, total, wide), BF),
            pltpu.VMEM((4, 64, LANES), BF),
            pltpu.VMEM((chunks, 4, 2, total, wide // 2), BF),
            pltpu.VMEM((8, total, LANES), BF),
            pltpu.VMEM((2, 2, 4, total, LANES), BF),
            pltpu.VMEM((units, width), BF),
            pltpu.VMEM((chunks, 2, LANES, wide // 2), BF),
            pltpu.VMEM((chunks, 2, LANES, wide // 2), BF),
            pltpu.VMEM((chunks, LANES, wide), F32),
            pltpu.VMEM((4, 8, LANES), F32),
            pltpu.VMEM((4, 8, LANES), F32),
            dma((3,)),
            dma((3,)),
            dma((chunks, 3)),
            dma((chunks, 3)),
            dma((2, 2, 4)),
            dma((2, 2, 4)),
            dma((chunks,)),
            dma((chunks,)),
            dma((chunks, 2)),
            dma((chunks, 2)),
            dma((chunks,)),
            dma((chunks,)),
            dma((chunks, 2)),
            dma((chunks, 2)),
            dma((3,)),
            dma((3,)),
            dma,
        ],
        compiler_params=pltpu.CompilerParams(
            collective_id=0, has_side_effects=True, vmem_limit_bytes=58 * 1024 * 1024
        ),
        cost_estimate=pl.CostEstimate(
            flops=4 * slots * units * width, bytes_accessed=2 * units * width, transcendentals=0
        ),
    )(
        grad_rows,
        grad_exponent.T,
        gate.astype(F32).reshape(1, tokens),
        routing.reshape(1, tokens),
        saved_hidden.reshape(slots, units),
        down_weight.reshape(units, width),
    )
    hidden_grad, weight_grad, gate_grad = finish(hidden_grad, weight_grad, gate_grad)
    return (hidden_grad[None, None], weight_grad[None], gate_grad.reshape(tokens))


def solution(mesh):
    in_specs = (
        P(("dp", "expert"), None),
        P(("dp", "expert"), None),
        P(("dp", "expert")),
        P(("dp", "expert"), None),
        P("dp", "expert", None, None),
        P("expert", None, None),
    )
    out_specs = (P("dp", "expert", None, None), P("expert", "dp", None), P(("dp", "expert")))

    def local(grad_rows, grad_exponent, gate, routing, saved_hidden, down_weight):
        args = (grad_rows, grad_exponent, gate, routing, saved_hidden, down_weight)
        tokens, width = grad_rows.shape
        slots, units = saved_hidden.shape[2:]
        fits = mesh.shape["dp"] == 8 and mesh.shape["expert"] == 4 and tokens == LANES
        fits = fits and slots == 4 * (MAIN + EXTRA) and units == 8 * LANES
        if fits and width == 4 * 7 * LANES:
            return local_fused(7, 2, *args)
        return local_general(*args)

    return jax.shard_map(local, mesh=mesh, in_specs=in_specs, out_specs=out_specs, check_vma=False)
```

```python
import functools

import jax
import jax.numpy as jnp
from jax import lax
from jax.experimental import pallas as pl
from jax.experimental.pallas import tpu as pltpu
from jax.sharding import PartitionSpec as P

MESH = pl.DeviceIdType.MESH
LANES = 128
MAIN = 32
EXTRA = 2
GATE_ROW = 56
BF = jnp.bfloat16
F32 = jnp.float32


def slot_table(route, experts, cap):
    onehot = (route[:, None] == jnp.arange(experts, dtype=jnp.int32)[None, :]).astype(jnp.int32)
    before = jnp.cumsum(onehot, axis=0) - onehot
    rank = jnp.sum(before * onehot, axis=1)
    slot = route * cap + rank
    return slot[:, None] == jnp.arange(experts * cap, dtype=jnp.int32)[None, :]


def scaled_rows(rows, exponent):
    count, width = rows.shape
    blocks = exponent.shape[1]
    factor = 1.0 / jnp.left_shift(jnp.ones_like(exponent), exponent).astype(jnp.float32)
    scaled = rows.astype(jnp.float32).reshape(count, blocks, width // blocks) * factor[:, :, None]
    return scaled.reshape(count, width).astype(jnp.bfloat16)


def local_general(grad_rows, grad_exponent, gate, routing, saved_hidden, down_weight):
    experts = lax.axis_size("expert")
    slots = saved_hidden.shape[2]
    cap = slots // experts
    width = grad_rows.shape[1]
    dy_local = scaled_rows(grad_rows, grad_exponent)
    place = slot_table(routing[:, 0], experts, cap)
    place_low = place.astype(jnp.bfloat16)
    sent = lax.dot_general(
        place_low, dy_local, (((0,), (0,)), ((), ())), preferred_element_type=jnp.float32
    )
    sent = sent.astype(jnp.bfloat16).reshape(experts, cap, width)
    gate_sent = jnp.dot(gate, place_low, preferred_element_type=jnp.float32)
    gate_sent = gate_sent.astype(jnp.bfloat16).reshape(experts, cap)
    arrived, arrived_gate = (
        lax.all_to_all(sent, "expert", split_axis=0, concat_axis=0, tiled=True),
        lax.all_to_all(gate_sent, "expert", split_axis=0, concat_axis=0, tiled=True),
    )
    rows = arrived.reshape(slots, width)
    gates = arrived_gate.reshape(slots).astype(jnp.float32)
    weight = down_weight[0]
    hidden = saved_hidden[0, 0]
    raw = lax.dot_general(
        rows, weight, (((1,), (1,)), ((), ())), preferred_element_type=jnp.float32
    )
    hidden_grad = (gates[:, None] * raw).astype(jnp.bfloat16)
    slot_grad = jnp.sum(hidden.astype(jnp.float32) * raw, axis=1)
    back = lax.all_to_all(
        slot_grad.reshape(experts, cap), "expert", split_axis=0, concat_axis=0, tiled=True
    )
    gate_grad = jnp.dot(
        place.astype(jnp.float32), back.reshape(slots), precision=lax.Precision.HIGHEST
    )
    weighted = (gates[:, None] * rows.astype(jnp.float32)).astype(jnp.bfloat16)
    weight_grad = lax.psum_scatter(
        lax.dot_general(
            hidden, weighted, (((0,), (0,)), ((), ())), preferred_element_type=jnp.float32
        ).astype(jnp.bfloat16),
        "dp",
        scatter_dimension=0,
        tiled=True,
    ).astype(jnp.float32)
    return (hidden_grad[None, None], weight_grad[None], gate_grad)


def iota(shape, axis):
    return lax.broadcasted_iota(jnp.int32, shape, axis)


def dot(a, b, dims=((1,), (0,)), precision=None):
    return lax.dot_general(a, b, (dims, ((), ())), preferred_element_type=F32, precision=precision)


def slot_of(i):
    main = i < 4 * MAIN
    j = i - 4 * MAIN
    source = jnp.where(main, i >> 5, j >> 1)
    rank = jnp.where(main, i & 31, MAIN + (j & 1))
    return source, rank


def pack_match(blocks, a, b):
    q = a & 63
    r = (q >= blocks).astype(jnp.int32)
    return (q < 2 * blocks) & (b == (q - blocks * r) * 16 + (a >> 6) * 2 + r)


def kernel(
    cap,
    chunks,
    ahead,
    rows_ref,
    exp_ref,
    gate_ref,
    route_ref,
    hidden_ref,
    weight_ref,
    hidden_grad_ref,
    weight_grad_ref,
    gate_grad_ref,
    dy,
    sent,
    sent_pack,
    rows,
    pack,
    gath,
    hblk,
    hg,
    wbuf,
    rs_send,
    rs_recv,
    wg,
    back_send,
    back_recv,
    pack_s,
    pack_r,
    z_s,
    z_r,
    h_s,
    h_r,
    core_s,
    core_r,
    nb_s,
    nb_r,
    relay_s,
    relay_r,
    rs_s,
    rs_r,
    back_s,
    back_r,
    w_sem,
):
    d = lax.axis_index("dp")
    me = lax.axis_index("expert")
    c = lax.rem(d, 2)
    x = lax.rem(lax.div(d, 2), 2)
    y = lax.div(d, 4)

    def dp_at(yy, xx, cc):
        return (yy * 2 + xx) * 2 + cc

    width = rows_ref.shape[1]
    wide = width // chunks
    blocks = wide // LANES
    half = wide // 2
    all_blocks = width // LANES
    total = 4 * MAIN + 16
    other = dp_at(y, x, 1 - c)
    near = (dp_at(y, 1 - x, c), dp_at(1 - y, x, c))
    near_other = (dp_at(y, 1 - x, 1 - c), dp_at(1 - y, x, 1 - c))
    peers_z = [lax.rem(me + o, 4) for o in (1, 2, 3)]

    load = pltpu.make_async_copy(weight_ref, wbuf, w_sem)
    load.start()

    barrier = pltpu.get_barrier_semaphore()
    for e in peers_z:
        pl.semaphore_signal(barrier, inc=1, device_id=(d, e), device_id_type=MESH)
    for p in (other,) + near + near_other:
        pl.semaphore_signal(barrier, inc=1, device_id=(p, me), device_id_type=MESH)

    def remote(src, dst, s, r, p, e):
        return pltpu.make_async_remote_copy(
            src_ref=src, dst_ref=dst, send_sem=s, recv_sem=r, device_id=(p, e), device_id_type=MESH
        )

    route = route_ref[...]
    onehot = iota((16, LANES), 0) == route
    onehot_low = onehot.astype(F32).astype(BF)
    earlier = (iota((LANES, LANES), 0) < iota((LANES, LANES), 1)).astype(F32).astype(BF)
    before = dot(onehot_low, earlier)
    rank = jnp.sum(jnp.where(onehot, before, 0.0), axis=0, keepdims=True).astype(jnp.int32)
    main_at = jnp.where(rank < MAIN, route * MAIN + rank, -1)
    extra_at = jnp.where(rank < MAIN, -1, route * EXTRA + rank - MAIN)
    place = (iota((LANES, LANES), 0) == main_at).astype(F32).astype(BF)
    place_extra = (iota((16, LANES), 0) == extra_at).astype(F32).astype(BF)
    rank_is = (iota((LANES, LANES), 0) == rank).astype(F32)
    gate_slots = dot(
        jnp.where(onehot, gate_ref[...].astype(F32).reshape(1, LANES), 0.0).astype(BF), rank_is.astype(BF), ((1,), (1,))
    ).astype(BF)

    factor = 1.0 / lax.shift_left(jnp.ones(exp_ref.shape, jnp.int32), exp_ref[...]).astype(F32)
    factor = jnp.concatenate([factor, jnp.zeros((32 - all_blocks, LANES), F32)], axis=0).T
    for b in range(all_blocks):
        columns = pl.ds(b * LANES, LANES)
        dy[:, columns] = (rows_ref[:, columns].astype(F32) * factor[:, b : b + 1]).astype(BF)
    extra = dot(place_extra, dy[...]).astype(BF)
    stacked = jnp.concatenate(
        [extra[:, b * LANES : (b + 1) * LANES] for b in range(all_blocks)], axis=0
    )
    at = (4 * 64, 16 * all_blocks)
    packing = pack_match(all_blocks, iota(at, 0), iota(at, 1)).astype(F32).astype(BF)
    at = iota((4 * 64, 16), 0)
    gate_row = (((at & 63) == GATE_ROW) & ((at >> 6) == iota((4 * 64, 16), 1))).astype(F32)
    tile = dot(packing, stacked) + dot(gate_row.astype(BF), gate_slots)
    sent_pack[...] = tile.astype(BF).reshape(4, 64, LANES)
    own_rows = pl.ds(pl.multiple_of(me * MAIN, MAIN), MAIN)
    z_copies = []

    def dispatch(k):
        sent[k] = dot(place, dy[:, k * wide : (k + 1) * wide]).astype(BF)
        if k == 0:
            pl.semaphore_wait(barrier, 8)
            for i, e in enumerate(peers_z):
                copy = remote(sent_pack.at[e], pack.at[me], pack_s.at[i], pack_r.at[i], d, e)
                copy.start()
                pack_copies.append(copy)
            pack[me] = sent_pack[me]
        group = []
        for i, e in enumerate(peers_z):
            copy = remote(
                sent.at[k, pl.ds(pl.multiple_of(e * MAIN, MAIN), MAIN)],
                rows.at[k, own_rows],
                z_s.at[k, i],
                z_r.at[k, i],
                d,
                e,
            )
            copy.start()
            group.append(copy)
        rows[k, own_rows, :] = sent[k, own_rows, :]
        z_copies.append(group)

    pack_copies = []
    for k in range(ahead):
        dispatch(k)

    slots = hidden_ref.shape[0]
    source, in_source = slot_of(iota((total, slots), 0))
    order = ((source < 4) & (iota((total, slots), 1) == source * cap + in_source))
    hidden = dot(order.astype(F32).astype(BF), hidden_ref[...]).astype(BF)
    for b in range(8):
        hblk[b] = hidden[:, b * LANES : (b + 1) * LANES]
    h_copies = []
    for t in range(2):
        for j, p in ((1, other), (2, near[t]), (3, near_other[t])):
            pc = lax.rem(p, 2)
            px = lax.rem(lax.div(p, 2), 2)
            py = lax.div(p, 4)
            partner = dp_at(1 - py, px, pc) if t == 0 else dp_at(py, 1 - px, pc)
            for b, block in enumerate((partner, p)):
                copy = remote(
                    hblk.at[block], hg.at[t, b, j], h_s.at[t, b, j], h_r.at[t, b, j], p, me
                )
                copy.start()
                h_copies.append(copy)
        for b, block in enumerate((near[1 - t], d)):
            hg[t, b, 0] = hblk[block]

    for copy in pack_copies:
        copy.wait_recv()
    at = (total, 4 * 64)
    source, _ = slot_of(iota(at, 0))
    pick = ((source < 4) & (iota(at, 1) == source * 64 + GATE_ROW)).astype(F32).astype(BF)
    spread = dot(pick, pack[...].reshape(4 * 64, LANES))
    source, in_source = slot_of(iota((total, LANES), 0))
    lane_is = (source < 4) & (iota((total, LANES), 1) == in_source)
    gates = jnp.sum(jnp.where(lane_is, spread, 0.0), axis=1, keepdims=True)

    core_copies, nb_copies, relay_copies, rs_copies = [], [], [], []
    raw = None

    def own_chunk(k):
        at = (16 * blocks, 4 * 64)
        unpacking = pack_match(all_blocks, iota(at, 1), iota(at, 0) + k * 16 * blocks)
        spread_rows = dot(unpacking.astype(F32).astype(BF), pack[...].reshape(4 * 64, LANES))
        for b in range(blocks):
            rows[k, 4 * MAIN :, b * LANES : (b + 1) * LANES] = spread_rows[
                b * 16 : (b + 1) * 16
            ].astype(BF)
        for copy in z_copies[k]:
            copy.wait_recv()
        if k + ahead < chunks:
            dispatch(k + ahead)
        pair = []
        for t in range(2):
            part = rows[k, :, t * half : (t + 1) * half].astype(F32)
            gath[k, 0, t] = (gates * part).astype(BF)
            copy = remote(
                gath.at[k, 0, t], gath.at[k, 2, t], nb_s.at[k, t], nb_r.at[k, t], near[t], me
            )
            copy.start()
            pair.append(copy)
        nb_copies.append(pair)
        copy = remote(gath.at[k, 0], gath.at[k, 1], core_s.at[k], core_r.at[k], other, me)
        copy.start()
        core_copies.append(copy)

    def relay_chunk(k):
        for copy in nb_copies[k]:
            copy.wait_recv()
        copy = remote(gath.at[k, 2], gath.at[k, 3], relay_s.at[k], relay_r.at[k], other, me)
        copy.start()
        relay_copies.append(copy)

    def partial_chunk(k):
        core_copies[k].wait_recv()
        relay_copies[k].wait_recv()
        pair = []
        for t in range(2):
            gathered = gath[k, :, t].reshape(4 * total, half)
            away = dot(hg[t, 0].reshape(4 * total, LANES), gathered, ((0,), (0,)))
            rs_send[k, t] = away.astype(BF)
            copy = remote(
                rs_send.at[k, t], rs_recv.at[k, t], rs_s.at[k, t], rs_r.at[k, t], near[1 - t], me
            )
            copy.start()
            pair.append(copy)
        rs_copies.append(pair)
        for t in range(2):
            gathered = gath[k, :, t].reshape(4 * total, half)
            wg[k, :, t * half : (t + 1) * half] = dot(
                hg[t, 1].reshape(4 * total, LANES), gathered, ((0,), (0,))
            )

    def add_chunk(k):
        for t in range(2):
            rs_copies[k][t].wait_recv()
            columns = pl.ds(t * half, half)
            target = pl.ds(k * wide + t * half, half)
            weight_grad_ref[:, target] = wg[k, :, columns] + rs_recv[k, t].astype(F32)

    for step in range(chunks + 2):
        if step < chunks:
            own_chunk(step)
        if 1 <= step <= chunks:
            relay_chunk(step - 1)
        if step < chunks:
            if step == 0:
                load.wait()
            term = dot(rows[step], wbuf[:, step * wide : (step + 1) * wide], ((1,), (1,)))
            raw = term if raw is None else raw + term
        if step == 1:
            for copy in h_copies:
                copy.wait_recv()
        if step == chunks - 1:
            slot_grad = jnp.sum(hidden.astype(F32) * raw, axis=1, keepdims=True)
            in_lane = jnp.where(lane_is, slot_grad, 0.0)
            tail = in_lane[4 * MAIN :]
            tail_at = iota(tail.shape, 0) >> 1
            for s in range(4):
                line = jnp.sum(in_lane[s * MAIN : (s + 1) * MAIN], axis=0, keepdims=True)
                line = line + jnp.sum(jnp.where(tail_at == s, tail, 0.0), axis=0, keepdims=True)
                back_send[s] = jnp.broadcast_to(line, (8, LANES))
            back_copies = []
            for i, e in enumerate(peers_z):
                copy = remote(back_send.at[e], back_recv.at[me], back_s.at[i], back_r.at[i], d, e)
                copy.start()
                back_copies.append(copy)
            back_recv[me] = back_send[me]
        if step >= 2:
            partial_chunk(step - 2)
        if step >= 5:
            add_chunk(step - 5)

    scaled = (gates * raw).astype(BF)
    source, in_source = slot_of(iota((slots, total), 1))
    order = ((source < 4) & (iota((slots, total), 0) == source * cap + in_source))
    hidden_grad_ref[...] = dot(order.astype(F32).astype(BF), scaled).astype(BF)

    for copy in back_copies:
        copy.wait_recv()
    taken = dot(
        back_recv[...].reshape(4 * 8, LANES), rank_is, precision=lax.Precision.HIGHEST
    )
    answer = jnp.zeros((1, LANES), F32)
    for e in range(4):
        answer = answer + jnp.where(route == e, taken[e * 8 : e * 8 + 1], 0.0)
    gate_grad_ref[...] = answer

    for k in range(chunks - 3, chunks):
        add_chunk(k)
    for copy in (
        pack_copies
        + [one for group in z_copies for one in group]
        + h_copies
        + core_copies
        + [one for pair in nb_copies for one in pair]
        + relay_copies
        + [one for pair in rs_copies for one in pair]
        + back_copies
    ):
        copy.wait_send()


PIECES = 8


def finish_kernel(*refs):
    sources, targets, sem = refs[:3], refs[3:6], refs[6]
    copies = []
    step = sources[1].shape[0] // PIECES
    for i in range(PIECES):
        at = pl.ds(i * step, step)
        copies.append(
            pltpu.make_async_copy(sources[1].at[at], targets[1].at[at], sem.at[i])
        )
    for i, j in ((0, PIECES), (2, PIECES + 1)):
        copies.append(pltpu.make_async_copy(sources[i], targets[i], sem.at[j]))
    for copy in copies:
        copy.start()
    for copy in copies:
        copy.wait()


def finish(*arrays):
    anywhere = pl.BlockSpec(memory_space=pl.ANY)
    return pl.pallas_call(
        finish_kernel,
        out_shape=tuple(jax.ShapeDtypeStruct(a.shape, a.dtype) for a in arrays),
        in_specs=[pl.BlockSpec(memory_space=pltpu.VMEM)] * 3,
        out_specs=(anywhere,) * 3,
        scratch_shapes=[pltpu.SemaphoreType.DMA((PIECES + 2,))],
        compiler_params=pltpu.CompilerParams(vmem_limit_bytes=16 * 1024 * 1024),
    )(*arrays)


def local_fused(chunks, ahead, grad_rows, grad_exponent, gate, routing, saved_hidden, down_weight):
    tokens, width = grad_rows.shape
    slots, units = saved_hidden.shape[2:]
    cap = slots // 4
    wide = width // chunks
    total = 4 * MAIN + 16
    dma = pltpu.SemaphoreType.DMA
    vmem = pl.BlockSpec(memory_space=pltpu.VMEM)
    anywhere = pl.BlockSpec(memory_space=pl.ANY)
    hidden_grad, weight_grad, gate_grad = pl.pallas_call(
        functools.partial(kernel, cap, chunks, ahead),
        out_shape=(
            pltpu.VMEM((slots, units), BF),
            pltpu.VMEM((units // 8, width), F32),
            pltpu.VMEM((1, tokens), F32),
        ),
        in_specs=[vmem] * 5 + [anywhere],
        out_specs=(vmem, vmem, vmem),
        scratch_shapes=[
            pltpu.VMEM((tokens, width), BF),
            pltpu.VMEM((chunks, 4 * MAIN, wide), BF),
            pltpu.VMEM((4, 64, LANES), BF),
            pltpu.VMEM((chunks, total, wide), BF),
            pltpu.VMEM((4, 64, LANES), BF),
            pltpu.VMEM((chunks, 4, 2, total, wide // 2), BF),
            pltpu.VMEM((8, total, LANES), BF),
            pltpu.VMEM((2, 2, 4, total, LANES), BF),
            pltpu.VMEM((units, width), BF),
            pltpu.VMEM((chunks, 2, LANES, wide // 2), BF),
            pltpu.VMEM((chunks, 2, LANES, wide // 2), BF),
            pltpu.VMEM((chunks, LANES, wide), F32),
            pltpu.VMEM((4, 8, LANES), F32),
            pltpu.VMEM((4, 8, LANES), F32),
            dma((3,)),
            dma((3,)),
            dma((chunks, 3)),
            dma((chunks, 3)),
            dma((2, 2, 4)),
            dma((2, 2, 4)),
            dma((chunks,)),
            dma((chunks,)),
            dma((chunks, 2)),
            dma((chunks, 2)),
            dma((chunks,)),
            dma((chunks,)),
            dma((chunks, 2)),
            dma((chunks, 2)),
            dma((3,)),
            dma((3,)),
            dma,
        ],
        compiler_params=pltpu.CompilerParams(
            collective_id=0, has_side_effects=True, vmem_limit_bytes=58 * 1024 * 1024
        ),
        cost_estimate=pl.CostEstimate(
            flops=4 * slots * units * width, bytes_accessed=2 * units * width, transcendentals=0
        ),
    )(
        grad_rows,
        grad_exponent.T,
        gate,
        routing.reshape(1, tokens),
        saved_hidden.reshape(slots, units),
        down_weight.reshape(units, width),
    )
    hidden_grad, weight_grad, gate_grad = finish(hidden_grad, weight_grad, gate_grad)
    return (hidden_grad[None, None], weight_grad[None], gate_grad.reshape(tokens))


def solution(mesh):
    in_specs = (
        P(("dp", "expert"), None),
        P(("dp", "expert"), None),
        P(("dp", "expert")),
        P(("dp", "expert"), None),
        P("dp", "expert", None, None),
        P("expert", None, None),
    )
    out_specs = (P("dp", "expert", None, None), P("expert", "dp", None), P(("dp", "expert")))

    def local(grad_rows, grad_exponent, gate, routing, saved_hidden, down_weight):
        args = (grad_rows, grad_exponent, gate, routing, saved_hidden, down_weight)
        tokens, width = grad_rows.shape
        slots, units = saved_hidden.shape[2:]
        fits = mesh.shape["dp"] == 8 and mesh.shape["expert"] == 4 and tokens == LANES
        fits = fits and slots == 4 * (MAIN + EXTRA) and units == 8 * LANES
        if fits and width == 4 * 7 * LANES:
            return local_fused(7, 2, *args)
        return local_general(*args)

    return jax.shard_map(local, mesh=mesh, in_specs=in_specs, out_specs=out_specs, check_vma=False)
```
